32 devices in a mesh: slab: 16 (over z, y, core), plane: 2 (over x).
Axes of the slice: x: 2, y: 2, z: 4, core: 2. Of those that a mesh axis runs over, the one named last changes fastest.
Arguments:
- rock_state: float32 [2, 32, 16, 512], P(None, 'slab', 'plane'), may hold values from -6 to 6
- rock_source: float32 [2, 32, 16, 512], P(None, 'slab', 'plane'), may hold values from -6 to 6
- transmissibility: bfloat16 [3, 32, 16, 512], P(None, 'slab', 'plane'), may hold values from 0.039794922 to 0.29882812
- cell_inverse: bfloat16 [4, 32, 16, 512], P(None, 'slab', 'plane'), may hold values from -0.06 to 0.3
- fracture_state: float32 [2, 32768], P(None, ('slab', 'plane')), may hold values from -6 to 6
- fracture_source: float32 [2, 32768], P(None, ('slab', 'plane')), may hold values from -6 to 6
- fracture_coupling: bfloat16 [256, 3, 128, 128], P(('slab', 'plane')), may hold values from -0.25 to 0.25
- fracture_inverse: bfloat16 [256, 128, 128], P(('slab', 'plane')), may hold values from -0.044194174 to 0.3941942
- fracture_neighbours: int32 [256, 3], P(('slab', 'plane')), may hold values from 0 to 255, as said below
- contact_cell: int32 [16, 32, 128], P('slab', 'plane'), may hold values from 0 to 8191
- contact_segment: int32 [16, 32, 128], P('slab', 'plane'), may hold values from 0 to 1023
- contact_weight: float32 [16, 32, 128], P('slab', 'plane'), may hold values from 0.3 to 1.5
- contact_count: int32 [16, 32], P('slab', 'plane'), may hold values from 32 to 128, as said below
Outputs:
- rock_final: float32 [2, 32, 16, 512], P(None, 'slab', 'plane')
- fracture_final: float32 [2, 32768], P(None, ('slab', 'plane'))
The draws below stay inside these ranges and needn't reach their ends.
Inputs may be any that keep to these rules, and one draw needn't show every extreme that they name: `contact_count`: live contact slots from one rock device to one fracture part of the same plane index; for every plane index some fracture part receives 128 live slots from every rock slab. `fracture_neighbours`: a block's neighbours are other blocks of its own part or of the parts one step away along slab with the same plane index.
All inputs are finite; a program needn't handle non-finite values.
Results may differ from the reference program's by a relative error of at most 0.0033.
Values may be sent and summed in bfloat16 or wider, within the bound.
A program may use at most 64 MiB of HBM per device.

```python
import math
import jax
import jax.numpy as jnp
from jax import lax

CZ = 2
CX = 8
NY = 512
FB_DEV = 8
NB = 128
NNB = 3
CAP = 128
ITERS = 3
NZ = 32
NX = 16
BLOCKS = 256
SEGS = 32768
N_SLAB = 16
N_PLANE = 2


def draw_cell_inverse(key, part):
    key_diag, key_off = jax.random.split(jax.random.fold_in(key, 11))
    shape = (2, NZ, NX, NY)
    diagonal = jnp.exp(jax.random.uniform(key_diag, shape, jnp.float32, math.log(0.1), math.log(0.295)))
    coupling = jax.random.uniform(key_off, shape, jnp.float32, -0.059, 0.059)
    return jnp.stack([diagonal[0], coupling[0], coupling[1], diagonal[1]]).astype(jnp.bfloat16)


def draw_fracture_inverse(key, part):
    key_diag, key_off = jax.random.split(jax.random.fold_in(key, 23))
    diagonal = jnp.exp(jax.random.uniform(key_diag, (BLOCKS, NB), jnp.float32, math.log(0.15), math.log(0.35)))
    spread = jnp.clip(jax.random.normal(key_off, (BLOCKS, NB, NB), jnp.float32), -4.0, 4.0) * 0.12
    matrix = spread / math.sqrt(NB) + diagonal[:, :, None] * jnp.eye(NB, dtype=jnp.float32)[None]
    return matrix.astype(jnp.bfloat16)


def draw_fracture_neighbours(key, part):
    key_off, key_pick = jax.random.split(jax.random.fold_in(key, 37))
    block_index = jnp.arange(BLOCKS, dtype=jnp.int32)
    owner_part = block_index // FB_DEV
    local_index = block_index % FB_DEV
    slab_index = owner_part // N_PLANE
    offset = jax.random.randint(key_off, (BLOCKS, NNB), -1, 2, jnp.int32)
    target = slab_index[:, None] + offset
    offset = jnp.where((target >= 0) & (target < N_SLAB), offset, 0)
    chosen = jax.random.randint(key_pick, (BLOCKS, NNB), 0, FB_DEV, jnp.int32)
    chosen = jnp.where((offset == 0) & (chosen == local_index[:, None]), (chosen + 1) % FB_DEV, chosen)
    return ((owner_part[:, None] + offset * N_PLANE) * FB_DEV + chosen).astype(jnp.int32)


def draw_contact_count(key, part):
    key_base, key_busy, key_force = jax.random.split(jax.random.fold_in(key, 53), 3)
    base_count = jax.random.randint(key_base, (N_SLAB, N_PLANE * N_SLAB), CAP // 4, CAP // 2 + 1, jnp.int32)
    busy_part = jax.random.randint(key_busy, (N_PLANE, N_SLAB), 0, 8, jnp.int32) == 0
    forced = jax.random.randint(key_force, (N_PLANE, 1), 0, N_SLAB, jnp.int32)
    busy_part = busy_part | (jnp.arange(N_SLAB, dtype=jnp.int32)[None, :] == forced)
    return jnp.where(busy_part.reshape(1, -1), CAP, base_count).astype(jnp.int32)


def touch_ends(result, own_key, least, largest):
    longest = result.shape.index(max(result.shape))
    spots = []
    for shift in (0, 1):
        where = [jax.random.randint(jax.random.fold_in(own_key, axis), (), 0, length) for axis, length in enumerate(result.shape)]
        where[longest] = (where[longest] + shift) % result.shape[longest]
        spots.append(tuple(where))
    return result.at[spots[0]].set(least).at[spots[1]].set(largest)


def steps_of(stream_key, extent, pieces, low, largest):
    loudness, own = 1.0, jax.random.fold_in(stream_key, 6)
    for axis_at, parts in pieces:
        draws = jnp.exp(jax.random.uniform(jax.random.fold_in(own, axis_at), (parts,), jnp.float32, low / len(pieces), largest / len(pieces)))
        loudness = loudness * jnp.repeat(draws, extent[axis_at] // parts).reshape([-1 if axis == axis_at else 1 for axis in range(len(extent))])
    return loudness


def scatter_about(stream_key, dims, deviation, limit, shards=(), held_as=jnp.bfloat16):
    result = deviation * jax.random.normal(stream_key, dims, jnp.float32)
    if shards:
        result = result * steps_of(stream_key, dims, shards, -0.22, 0.18)
    return jnp.clip(result, -limit, limit).astype(held_as)


def setup_inputs(seed: int = 0) -> dict:
    seeds = jax.random.split(jax.random.key(seed), 14)
    return {
        "rock_state": scatter_about(seeds[0], (2, NZ, NX, NY), 1.0, 6.0, ((1, 16), (2, 2)), jnp.float32),
        "rock_source": scatter_about(seeds[1], (2, NZ, NX, NY), 1.0, 6.0, ((1, 16), (2, 2)), jnp.float32),
        "transmissibility": jnp.clip(jnp.exp(math.log(0.29882812) - 2.0161293 * jax.random.uniform(seeds[2], (3, NZ, NX, NY), jnp.float32) ** steps_of(seeds[2], (3, NZ, NX, NY), ((1, 16), (2, 2)), -0.2, 0.2)), 0.039794922, 0.29882812).astype(jnp.bfloat16),
        "cell_inverse": draw_cell_inverse(jax.random.fold_in(seeds[13], 71), 0),
        "fracture_state": scatter_about(seeds[4], (2, SEGS), 1.0, 6.0, ((1, 32),), jnp.float32),
        "fracture_source": scatter_about(seeds[5], (2, SEGS), 1.0, 6.0, ((1, 32),), jnp.float32),
        "fracture_coupling": scatter_about(seeds[6], (BLOCKS, NNB, NB, NB), (4 * NB) ** -0.5, 0.25, ((0, 32),)),
        "fracture_inverse": draw_fracture_inverse(jax.random.fold_in(seeds[13], 71), 0),
        "fracture_neighbours": draw_fracture_neighbours(jax.random.fold_in(seeds[13], 71), 0),
        "contact_cell": touch_ends(jax.random.randint(seeds[9], (N_SLAB, N_PLANE * N_SLAB, CAP), 0, CZ * CX * NY), jax.random.fold_in(seeds[9], 1), 0, (CZ * CX * NY) - 1).astype(jnp.int32),
        "contact_segment": touch_ends(jax.random.randint(seeds[10], (N_SLAB, N_PLANE * N_SLAB, CAP), 0, FB_DEV * NB), jax.random.fold_in(seeds[10], 1), 0, (FB_DEV * NB) - 1).astype(jnp.int32),
        "contact_weight": jnp.clip(jnp.exp(math.log(1.5) - 1.60943787 * jax.random.uniform(seeds[11], (N_SLAB, N_PLANE * N_SLAB, CAP), jnp.float32) ** steps_of(seeds[11], (N_SLAB, N_PLANE * N_SLAB, CAP), ((0, 16), (1, 2)), -0.2, 0.2)), 0.3, 1.5),
        "contact_count": draw_contact_count(jax.random.fold_in(seeds[13], 71), 0),
    }


def couple_group(pair):
    matrices, states = pair
    return jnp.einsum("bkij,bkfj->bfi", matrices.astype(jnp.float32), states.astype(jnp.float32))


def invert_group(pair):
    matrices, states = pair
    return jnp.einsum("bij,bfj->bfi", matrices.astype(jnp.float32), states.astype(jnp.float32))


def reference(rock_state, rock_source, transmissibility, cell_inverse, fracture_state, fracture_source, fracture_coupling, fracture_inverse, fracture_neighbours, contact_cell, contact_segment, contact_weight, contact_count):
    source_slab = jnp.arange(N_SLAB, dtype=jnp.int32)[:, None, None]
    column = jnp.arange(N_PLANE * N_SLAB, dtype=jnp.int32)[None, :, None]
    plane_index = column // N_SLAB
    target_slab = column % N_SLAB
    layer_z = contact_cell // (CX * NY)
    layer_x = (contact_cell // NY) % CX
    layer_y = contact_cell % NY
    global_cell = (((source_slab * CZ + layer_z) * NX + plane_index * CX + layer_x) * NY + layer_y).reshape(-1).astype(jnp.int32)
    global_segment = ((target_slab * N_PLANE + plane_index) * FB_DEV * NB + contact_segment).reshape(-1).astype(jnp.int32)
    slot_index = jnp.arange(CAP, dtype=jnp.int32)[None, None, :]
    slot_weight = jnp.where(slot_index < contact_count[:, :, None], contact_weight, jnp.zeros_like(contact_weight)).reshape(-1)
    coef = transmissibility.astype(jnp.float32)
    coef_next = jnp.stack([
        jnp.pad(coef[0, 1:], ((0, 1), (0, 0), (0, 0))),
        jnp.pad(coef[1, :, 1:], ((0, 0), (0, 1), (0, 0))),
        jnp.pad(coef[2, :, :, 1:], ((0, 0), (0, 0), (0, 1)))])
    inverse = cell_inverse.astype(jnp.float32)
    groups = BLOCKS // FB_DEV
    coupling_groups = fracture_coupling.reshape(groups, FB_DEV, NNB, NB, NB)
    inverse_groups = fracture_inverse.reshape(groups, FB_DEV, NB, NB)
    cell_total = NZ * NX * NY
    source_blocks = fracture_source.reshape(2, BLOCKS, NB).transpose(1, 0, 2)
    rock_now = rock_state
    fracture_now = fracture_state
    for sweep_index in range(ITERS):
        rock_flat = rock_now.reshape(2, -1)
        leak_fracture = jax.ops.segment_sum((slot_weight * rock_flat[:, global_cell]).T, global_segment, num_segments=SEGS).T
        leak_rock = jax.ops.segment_sum((slot_weight * fracture_now[:, global_segment]).T, global_cell, num_segments=cell_total).T.reshape(rock_now.shape)
        fracture_low = fracture_now.astype(jnp.bfloat16).reshape(2, BLOCKS, NB).transpose(1, 0, 2)
        gathered = fracture_low[fracture_neighbours]
        coupled = lax.map(couple_group, (coupling_groups, gathered.reshape(groups, FB_DEV, NNB, 2, NB))).reshape(BLOCKS, 2, NB)
        leak_blocks = leak_fracture.reshape(2, BLOCKS, NB).transpose(1, 0, 2)
        fracture_rhs = (source_blocks + leak_blocks - coupled).astype(jnp.bfloat16)
        fracture_next = lax.map(invert_group, (inverse_groups, fracture_rhs.reshape(groups, FB_DEV, 2, NB)))
        fracture_next = fracture_next.reshape(BLOCKS, 2, NB).transpose(1, 0, 2).reshape(2, -1)
        padded = jnp.pad(rock_now, ((0, 0), (1, 1), (1, 1), (1, 1)))
        near_sum = coef[0] * padded[:, :-2, 1:-1, 1:-1] + coef[1] * padded[:, 1:-1, :-2, 1:-1] + coef[2] * padded[:, 1:-1, 1:-1, :-2]
        near_sum = near_sum + coef_next[0] * padded[:, 2:, 1:-1, 1:-1] + coef_next[1] * padded[:, 1:-1, 2:, 1:-1] + coef_next[2] * padded[:, 1:-1, 1:-1, 2:]
        rock_rhs = rock_source + near_sum + leak_rock
        rock_now = jnp.stack([inverse[0] * rock_rhs[0] + inverse[1] * rock_rhs[1], inverse[2] * rock_rhs[0] + inverse[3] * rock_rhs[1]])
        fracture_now = fracture_next
    return rock_now, fracture_now
```

```python
import functools

import jax
import jax.numpy as jnp
from jax import lax
from jax.experimental import pallas as pl
from jax.experimental.pallas import tpu as pltpu
from jax.sharding import PartitionSpec as P

ITERS = 3
LANES = 128
F32 = jnp.float32
BF16 = jnp.bfloat16
MESH = pl.DeviceIdType.MESH
NT = (((1,), (1,)), ((), ()))


def split(value):
    high = value.astype(BF16)
    low = (value - high.astype(F32)).astype(BF16)
    return high, low


def kernel(
    n,
    planes,
    rock_ref,
    source_ref,
    trans_ref,
    inverse_ref,
    frac_ref,
    frac_source_ref,
    coupling_ref,
    frac_inverse_ref,
    near_ref,
    cell_ref,
    segment_ref,
    weight_ref,
    count_ref,
    rock_out,
    frac_out,
    cell_hot,
    cell_mask,
    seg_hot,
    seg_mask,
    weights,
    seg_send,
    seg_recv,
    slot_send,
    slot_recv,
    up_send,
    down_send,
    up_recv,
    down_recv,
    right_send,
    left_send,
    right_recv,
    left_recv,
    frac_send,
    below_recv,
    above_recv,
    seg_sems,
    slot_sems,
    halo_send_sems,
    halo_recv_sems,
):
    slab = lax.axis_index("slab")
    plane = lax.axis_index("plane")
    blocks = coupling_ref.shape[0]
    has_below, has_above = slab > 0, slab < n - 1
    has_left, has_right = plane > 0, plane < planes - 1

    barrier = pltpu.get_barrier_semaphore()

    def greet(step, carry):
        pl.semaphore_signal(
            barrier, inc=1, device_id={"slab": lax.rem(slab + step, n)}, device_id_type=MESH
        )
        return carry

    lax.fori_loop(1, n, greet, 0)

    @pl.when(has_left)
    def _():
        pl.semaphore_signal(barrier, inc=1, device_id={"plane": plane - 1}, device_id_type=MESH)

    @pl.when(has_right)
    def _():
        pl.semaphore_signal(barrier, inc=1, device_id={"plane": plane + 1}, device_id_type=MESH)

    for s in range(n):
        seg_send[s] = segment_ref[0, s : s + 1, :]

    @pl.when(jnp.logical_not(has_below))
    def _():
        up_recv[...] = jnp.zeros_like(up_recv)
        below_recv[...] = jnp.zeros_like(below_recv)

    @pl.when(jnp.logical_not(has_above))
    def _():
        down_recv[...] = jnp.zeros_like(down_recv)
        above_recv[...] = jnp.zeros_like(above_recv)

    @pl.when(jnp.logical_not(has_left))
    def _():
        right_recv[...] = jnp.zeros_like(right_recv)

    @pl.when(jnp.logical_not(has_right))
    def _():
        left_recv[...] = jnp.zeros_like(left_recv)

    neighbours_x = has_left.astype(jnp.int32) + has_right.astype(jnp.int32)
    pl.semaphore_wait(barrier, n - 1 + neighbours_x)

    def send_segments(step, carry):
        peer = lax.rem(slab + step, n)
        pltpu.make_async_remote_copy(
            seg_send.at[peer], seg_recv.at[slab], seg_sems.at[0], seg_sems.at[1],
            device_id={"slab": peer}, device_id_type=MESH,
        ).start()
        return carry

    lax.fori_loop(1, n, send_segments, 0)
    seg_recv[slab] = seg_send[slab]

    def halo_copy(index, sweep, sent, landed, target):
        return pltpu.make_async_remote_copy(
            sent.at[sweep], landed.at[sweep],
            halo_send_sems.at[index, sweep], halo_recv_sems.at[index, sweep],
            device_id=target, device_id_type=MESH,
        )

    def halo_copies(sweep):
        above, below = {"slab": slab + 1}, {"slab": slab - 1}
        right, left = {"plane": plane + 1}, {"plane": plane - 1}
        return [
            (has_above, has_below, halo_copy(0, sweep, up_send, up_recv, above)),
            (has_below, has_above, halo_copy(1, sweep, down_send, down_recv, below)),
            (has_right, has_left, halo_copy(2, sweep, right_send, right_recv, right)),
            (has_left, has_right, halo_copy(3, sweep, left_send, left_recv, left)),
            (has_above, has_below, halo_copy(4, sweep, frac_send, below_recv, above)),
            (has_below, has_above, halo_copy(5, sweep, frac_send, above_recv, below)),
        ]

    def start_when(flag, copy):
        @pl.when(flag)
        def _():
            copy.start()

    def landed_when(flag, copy):
        @pl.when(flag)
        def _():
            copy.wait_recv()

    def sent_when(flag, copy):
        @pl.when(flag)
        def _():
            copy.wait_send()

    coef = [[trans_ref[d, z].astype(F32) for z in range(2)] for d in range(3)]
    x_rows = coef[0][0].shape[0]
    width = coef[0][0].shape[1]
    lane = lax.broadcasted_iota(jnp.int32, (x_rows, width), 1)
    row = lax.broadcasted_iota(jnp.int32, (x_rows, width), 0)
    parts_y = width // LANES

    def send_halos(sweep, rock, frac):
        for f in range(2):
            up_send[sweep, f] = rock[f][1]
            down_send[sweep, f] = coef[0][0] * rock[f][0]
            for z in range(2):
                at = slice(f * 2 + z, f * 2 + z + 1)
                right_send[sweep, at] = rock[f][z][x_rows - 1 :]
                left_send[sweep, at] = coef[1][z][:1] * rock[f][z][:1]
        frac_send[sweep] = frac.astype(BF16)
        for sends, _, copy in halo_copies(sweep):
            start_when(sends, copy)

    rock = [[rock_ref[f, z] for z in range(2)] for f in range(2)]

    def to_blocks(ref):
        return jnp.concatenate(
            [ref[f : f + 1, b * LANES : (b + 1) * LANES] for f in range(2) for b in range(blocks)],
            axis=0,
        )

    frac = to_blocks(frac_ref)
    frac_source = to_blocks(frac_source_ref)
    send_halos(0, rock, frac)

    slot_lane = lax.broadcasted_iota(jnp.int32, (1, LANES), 1)
    table_rows = 2 * x_rows * parts_y
    hot_row = lax.broadcasted_iota(jnp.int32, (LANES, LANES), 0)
    mask_row = lax.broadcasted_iota(jnp.int32, (table_rows, LANES), 0)
    block_row = lax.broadcasted_iota(jnp.int32, (blocks, LANES), 0)
    y_shift = width.bit_length() - 1
    for s in range(n):
        at = slice(s * LANES, (s + 1) * LANES)
        cell = cell_ref[0, s : s + 1, :]
        hot = jnp.where(hot_row == (cell & (LANES - 1)), 1.0, 0.0).astype(BF16)
        cell_hot[:LANES, at] = hot
        cell_hot[LANES:, at] = hot
        y_part = (cell & (width - 1)) >> 7
        table_row = y_part * (2 * x_rows) + (cell >> y_shift)
        cell_mask[:, at] = jnp.where(mask_row == table_row, 1.0, 0.0)
        weights[s : s + 1, :] = jnp.where(
            slot_lane < count_ref[0, s], weight_ref[0, s : s + 1, :], 0.0
        )

    def pick_rock(sweep, rock):
        table = jnp.concatenate(
            [
                rock[f][z][:, p * LANES : (p + 1) * LANES]
                for f in range(2) for p in range(parts_y) for z in range(2)
            ],
            axis=0,
        )
        left = jnp.concatenate(split(table), axis=1)
        for c in range(n // 2):
            at = slice(c * 256, (c + 1) * 256)
            spread = jnp.dot(left, cell_hot[:, at], preferred_element_type=F32)
            mask = cell_mask[:, at]
            for f in range(2):
                picked = jnp.sum(
                    spread[f * table_rows : (f + 1) * table_rows] * mask, axis=0, keepdims=True
                )
                for h in range(2):
                    s = 2 * c + h
                    slot_send[sweep, s, f : f + 1] = (
                        picked[:, h * LANES : (h + 1) * LANES] * weights[s : s + 1]
                    )

    def pick_frac(sweep, frac):
        left = jnp.concatenate(split(frac), axis=1)
        for c in range(n // 2):
            at = slice(c * 256, (c + 1) * 256)
            spread = jnp.dot(left, seg_hot[:, at], preferred_element_type=F32)
            mask = seg_mask[:, at]
            for f in range(2):
                picked = jnp.sum(
                    spread[f * blocks : (f + 1) * blocks] * mask, axis=0, keepdims=True
                )
                for h in range(2):
                    slot_send[sweep, 2 * c + h, 2 + f : 3 + f] = picked[
                        :, h * LANES : (h + 1) * LANES
                    ]

    def send_slots(sweep):
        def body(step, carry):
            peer = lax.rem(slab + step, n)
            pltpu.make_async_remote_copy(
                slot_send.at[sweep, peer], slot_recv.at[sweep, slab],
                slot_sems.at[0, sweep], slot_sems.at[1, sweep],
                device_id={"slab": peer}, device_id_type=MESH,
            ).start()
            return carry

        lax.fori_loop(1, n, body, 0)
        slot_recv[sweep, slab] = slot_send[sweep, slab]

    def place(values, mask_ref, hot_ref, count):
        pieces = []
        for s in range(n):
            mask = mask_ref[:, s * LANES : (s + 1) * LANES]
            parts = [split(value) for value in values(s)]
            column = [
                (parts[f][h].astype(F32) * mask).astype(BF16) for h in range(2) for f in range(2)
            ]
            pieces.append(jnp.concatenate(column, axis=0))
        left = jnp.concatenate(pieces, axis=1)
        result = lax.dot_general(left, hot_ref[:LANES, :], NT, preferred_element_type=F32)
        return result[: 2 * count] + result[2 * count :]

    pick_rock(0, rock)

    my_part = slab * planes + plane
    q = lax.broadcasted_iota(jnp.int32, (2 * blocks, 6 * blocks), 1)
    f_row = lax.broadcasted_iota(jnp.int32, (2 * blocks, 6 * blocks), 0) // blocks
    rim = []
    for k in range(3):
        near = near_ref[:, k : k + 1]
        owner = near // blocks
        side = jnp.where(owner > my_part, 2, jnp.where(owner < my_part, 0, 1))
        code = side * (2 * blocks) + near % blocks
        code = jnp.concatenate([code, code], axis=0)
        rim.append(jnp.where(q == code + f_row * blocks, 1.0, 0.0).astype(BF16))
    rim = jnp.concatenate(rim, axis=0)
    block_of_row = lax.broadcasted_iota(jnp.int32, (2 * blocks, LANES), 0) % blocks

    for half, sem in ((seg_send, 0), (seg_recv, 1)):
        pltpu.make_async_copy(
            half.at[pl.ds(0, n - 1)], half.at[pl.ds(0, n - 1)], seg_sems.at[sem]
        ).wait()
    for s in range(n):
        at = slice(s * LANES, (s + 1) * LANES)
        segment = seg_recv[s]
        hot = jnp.where(hot_row == (segment & (LANES - 1)), 1.0, 0.0).astype(BF16)
        seg_hot[:LANES, at] = hot
        seg_hot[LANES:, at] = hot
        seg_mask[:, at] = jnp.where(block_row == (segment >> 7), 1.0, 0.0)

    def by_block(left, right):
        total = jnp.zeros((2 * blocks, LANES), F32)
        for b in range(0, blocks, 2):
            matrices = jnp.concatenate([right(b), right(b + 1)], axis=0)
            result = lax.dot_general(left, matrices, NT, preferred_element_type=F32)
            total = jnp.where(block_of_row == b, result[:, :LANES], total)
            total = jnp.where(block_of_row == b + 1, result[:, LANES:], total)
        return total

    for sweep in range(ITERS):
        if sweep:
            pick_rock(sweep, rock)
        pick_frac(sweep, frac)
        send_slots(sweep)

        near_sum = [[None, None], [None, None]]
        for f in range(2):
            for z in range(2):
                value = rock[f][z]
                product_y = coef[2][z] * value
                product_x = coef[1][z] * value
                total = source_ref[f, z]
                total += coef[2][z] * jnp.where(lane == 0, 0.0, pltpu.roll(value, 1, 1))
                total += jnp.where(lane == width - 1, 0.0, pltpu.roll(product_y, width - 1, 1))
                total += coef[1][z] * jnp.where(row == 0, 0.0, pltpu.roll(value, 1, 0))
                total += jnp.where(
                    row == x_rows - 1, 0.0, pltpu.roll(product_x, x_rows - 1, 0)
                )
                near_sum[f][z] = total
            near_sum[f][0] += coef[0][1] * rock[f][1]
            near_sum[f][1] += coef[0][1] * rock[f][0]

        copies = halo_copies(sweep)
        for _, lands, copy in copies:
            landed_when(lands, copy)
        for f in range(2):
            near_sum[f][0] += coef[0][0] * up_recv[sweep, f]
            near_sum[f][1] += down_recv[sweep, f]
            for z in range(2):
                at = slice(f * 2 + z, f * 2 + z + 1)
                near_sum[f][z] += jnp.where(
                    row == 0, coef[1][z] * right_recv[sweep, at],
                    jnp.where(row == x_rows - 1, left_recv[sweep, at], 0.0),
                )
        around = jnp.concatenate(
            [below_recv[sweep], frac.astype(BF16), above_recv[sweep]], axis=0
        )
        gathered = jnp.dot(rim, around, preferred_element_type=F32).astype(BF16)
        gathered = jnp.concatenate(
            [gathered[k * 2 * blocks : (k + 1) * 2 * blocks] for k in range(3)], axis=1
        )
        coupled = by_block(
            gathered, lambda b: jnp.concatenate([coupling_ref[b, k] for k in range(3)], axis=1)
        )

        pltpu.make_async_copy(
            slot_recv.at[sweep, pl.ds(0, n - 1)], slot_recv.at[sweep, pl.ds(0, n - 1)],
            slot_sems.at[1, sweep],
        ).wait()
        leak_frac = place(
            lambda s: [slot_recv[sweep, s, f : f + 1] for f in range(2)], seg_mask, seg_hot, blocks
        )
        frac_rhs = (frac_source + leak_frac - coupled).astype(BF16)
        frac = by_block(frac_rhs, lambda b: frac_inverse_ref[b])
        leak_rock = place(
            lambda s: [
                weights[s : s + 1] * slot_recv[sweep, s, 2 + f : 3 + f] for f in range(2)
            ],
            cell_mask, cell_hot, table_rows,
        )
        rhs = [[None, None], [None, None]]
        for f in range(2):
            for z in range(2):
                first = [f * table_rows + (p * 2 + z) * x_rows for p in range(parts_y)]
                rhs[f][z] = near_sum[f][z] + jnp.concatenate(
                    [leak_rock[i : i + x_rows] for i in first], axis=1
                )
        rock = [
            [
                inverse_ref[2 * g, z].astype(F32) * rhs[0][z]
                + inverse_ref[2 * g + 1, z].astype(F32) * rhs[1][z]
                for z in range(2)
            ]
            for g in range(2)
        ]
        if sweep < ITERS - 1:
            send_halos(sweep + 1, rock, frac)

    for f in range(2):
        for z in range(2):
            rock_out[f, z] = rock[f][z]
        for b in range(blocks):
            frac_out[f : f + 1, b * LANES : (b + 1) * LANES] = frac[
                f * blocks + b : f * blocks + b + 1
            ]
    for sweep in range(ITERS):
        for sends, _, copy in halo_copies(sweep):
            sent_when(sends, copy)
        pltpu.make_async_copy(
            slot_send.at[sweep, pl.ds(0, n - 1)], slot_send.at[sweep, pl.ds(0, n - 1)],
            slot_sems.at[0, sweep],
        ).wait()


def shards(n, planes, *operands):
    rock_state = operands[0]
    blocks = operands[6].shape[0]
    _, layers, x_rows, width = rock_state.shape
    table_rows = layers * x_rows * width // LANES
    vmem = pl.BlockSpec(memory_space=pltpu.VMEM)
    smem = pl.BlockSpec(memory_space=pltpu.SMEM)
    slots = n * LANES
    return pl.pallas_call(
        functools.partial(kernel, n, planes),
        out_shape=(
            jax.ShapeDtypeStruct(rock_state.shape, F32),
            jax.ShapeDtypeStruct(operands[4].shape, F32),
        ),
        in_specs=[vmem] * 12 + [smem],
        out_specs=(vmem, vmem),
        scratch_shapes=[
            pltpu.VMEM((2 * LANES, slots), BF16),
            pltpu.VMEM((table_rows, slots), F32),
            pltpu.VMEM((2 * LANES, slots), BF16),
            pltpu.VMEM((blocks, slots), F32),
            pltpu.VMEM((n, LANES), F32),
            pltpu.VMEM((n, 1, LANES), jnp.int32),
            pltpu.VMEM((n, 1, LANES), jnp.int32),
            pltpu.VMEM((ITERS, n, 4, LANES), F32),
            pltpu.VMEM((ITERS, n, 4, LANES), F32),
            pltpu.VMEM((ITERS, 2, x_rows, width), F32),
            pltpu.VMEM((ITERS, 2, x_rows, width), F32),
            pltpu.VMEM((ITERS, 2, x_rows, width), F32),
            pltpu.VMEM((ITERS, 2, x_rows, width), F32),
            pltpu.VMEM((ITERS, 2 * layers, width), F32),
            pltpu.VMEM((ITERS, 2 * layers, width), F32),
            pltpu.VMEM((ITERS, 2 * layers, width), F32),
            pltpu.VMEM((ITERS, 2 * layers, width), F32),
            pltpu.VMEM((ITERS, 2 * blocks, LANES), BF16),
            pltpu.VMEM((ITERS, 2 * blocks, LANES), BF16),
            pltpu.VMEM((ITERS, 2 * blocks, LANES), BF16),
            pltpu.SemaphoreType.DMA((2,)),
            pltpu.SemaphoreType.DMA((2, ITERS)),
            pltpu.SemaphoreType.DMA((6, ITERS)),
            pltpu.SemaphoreType.DMA((6, ITERS)),
        ],
        compiler_params=pltpu.CompilerParams(
            collective_id=0, has_side_effects=True, vmem_limit_bytes=48 * 1024 * 1024
        ),
    )(*operands)


def solution(mesh):
    return jax.shard_map(
        functools.partial(shards, mesh.shape["slab"], mesh.shape["plane"]),
        mesh=mesh,
        in_specs=(
            P(None, "slab", "plane", None),
            P(None, "slab", "plane", None),
            P(None, "slab", "plane", None),
            P(None, "slab", "plane", None),
            P(None, ("slab", "plane")),
            P(None, ("slab", "plane")),
            P(("slab", "plane"), None, None, None),
            P(("slab", "plane"), None, None),
            P(("slab", "plane"), None),
            P("slab", "plane", None),
            P("slab", "plane", None),
            P("slab", "plane", None),
            P("slab", "plane"),
        ),
        out_specs=(P(None, "slab", "plane", None), P(None, ("slab", "plane"))),
        check_vma=False,
    )
```

```python
import functools

import jax
import jax.numpy as jnp
from jax import lax
from jax.experimental import pallas as pl
from jax.experimental.pallas import tpu as pltpu
from jax.sharding import PartitionSpec as P

ITERS = 3
LANES = 128
F32 = jnp.float32
BF16 = jnp.bfloat16
MESH = pl.DeviceIdType.MESH
NT = (((1,), (1,)), ((), ()))


def split(value):
    high = value.astype(BF16)
    low = (value - high.astype(F32)).astype(BF16)
    return high, low


def kernel(n, planes, *refs):
    arrays, (rock_out, frac_out), held = refs[:13], refs[13:15], refs[15:28]
    (
        cell_hot,
        cell_mask,
        seg_hot,
        seg_mask,
        weights,
        seg_send,
        seg_recv,
        slot_send,
        slot_recv,
        up_send,
        down_send,
        up_recv,
        down_recv,
        right_send,
        left_send,
        right_recv,
        left_recv,
        frac_send,
        below_recv,
        above_recv,
        seg_sems,
        slot_sems,
        halo_send_sems,
        halo_recv_sems,
        load_sems,
    ) = refs[28:]
    (
        rock_ref,
        source_ref,
        trans_ref,
        inverse_ref,
        frac_ref,
        frac_source_ref,
        coupling_ref,
        frac_inverse_ref,
        near_ref,
        cell_ref,
        segment_ref,
        weight_ref,
        count_ref,
    ) = held
    loads = [
        pltpu.make_async_copy(arrays[i], held[i], load_sems.at[i]) for i in range(len(arrays))
    ]
    for i in (10, 0, 2, 4, 9, 12, 11, 8, 1, 5, 6, 7, 3):
        loads[i].start()

    def loaded(*which):
        for i in which:
            loads[i].wait()

    slab = lax.axis_index("slab")
    plane = lax.axis_index("plane")
    blocks = coupling_ref.shape[0]
    has_below, has_above = slab > 0, slab < n - 1
    has_left, has_right = plane > 0, plane < planes - 1

    barrier = pltpu.get_barrier_semaphore()

    def greet(step, carry):
        pl.semaphore_signal(
            barrier, inc=1, device_id={"slab": lax.rem(slab + step, n)}, device_id_type=MESH
        )
        return carry

    lax.fori_loop(1, n, greet, 0)

    @pl.when(has_left)
    def _():
        pl.semaphore_signal(barrier, inc=1, device_id={"plane": plane - 1}, device_id_type=MESH)

    @pl.when(has_right)
    def _():
        pl.semaphore_signal(barrier, inc=1, device_id={"plane": plane + 1}, device_id_type=MESH)

    loaded(10)
    for s in range(n):
        seg_send[s] = segment_ref[0, s : s + 1, :]

    @pl.when(jnp.logical_not(has_below))
    def _():
        up_recv[...] = jnp.zeros_like(up_recv)
        below_recv[...] = jnp.zeros_like(below_recv)

    @pl.when(jnp.logical_not(has_above))
    def _():
        down_recv[...] = jnp.zeros_like(down_recv)
        above_recv[...] = jnp.zeros_like(above_recv)

    @pl.when(jnp.logical_not(has_left))
    def _():
        right_recv[...] = jnp.zeros_like(right_recv)

    @pl.when(jnp.logical_not(has_right))
    def _():
        left_recv[...] = jnp.zeros_like(left_recv)

    neighbours_x = has_left.astype(jnp.int32) + has_right.astype(jnp.int32)
    pl.semaphore_wait(barrier, n - 1 + neighbours_x)

    def send_segments(step, carry):
        peer = lax.rem(slab + step, n)
        pltpu.make_async_remote_copy(
            seg_send.at[peer], seg_recv.at[slab], seg_sems.at[0], seg_sems.at[1],
            device_id={"slab": peer}, device_id_type=MESH,
        ).start()
        return carry

    lax.fori_loop(1, n, send_segments, 0)
    seg_recv[slab] = seg_send[slab]

    def halo_copy(index, sweep, sent, landed, target):
        return pltpu.make_async_remote_copy(
            sent.at[sweep], landed.at[sweep],
            halo_send_sems.at[index, sweep], halo_recv_sems.at[index, sweep],
            device_id=target, device_id_type=MESH,
        )

    def halo_copies(sweep):
        above, below = {"slab": slab + 1}, {"slab": slab - 1}
        right, left = {"plane": plane + 1}, {"plane": plane - 1}
        return [
            (has_above, has_below, halo_copy(0, sweep, up_send, up_recv, above)),
            (has_below, has_above, halo_copy(1, sweep, down_send, down_recv, below)),
            (has_right, has_left, halo_copy(2, sweep, right_send, right_recv, right)),
            (has_left, has_right, halo_copy(3, sweep, left_send, left_recv, left)),
            (has_above, has_below, halo_copy(4, sweep, frac_send, below_recv, above)),
            (has_below, has_above, halo_copy(5, sweep, frac_send, above_recv, below)),
        ]

    def start_when(flag, copy):
        @pl.when(flag)
        def _():
            copy.start()

    def landed_when(flag, copy):
        @pl.when(flag)
        def _():
            copy.wait_recv()

    def sent_when(flag, copy):
        @pl.when(flag)
        def _():
            copy.wait_send()

    loaded(2, 0, 4)
    coef = [[trans_ref[d, z].astype(F32) for z in range(2)] for d in range(3)]
    x_rows = coef[0][0].shape[0]
    width = coef[0][0].shape[1]
    lane = lax.broadcasted_iota(jnp.int32, (x_rows, width), 1)
    row = lax.broadcasted_iota(jnp.int32, (x_rows, width), 0)
    parts_y = width // LANES

    def send_halos(sweep, rock, frac):
        for f in range(2):
            up_send[sweep, f] = rock[f][1]
            down_send[sweep, f] = coef[0][0] * rock[f][0]
            for z in range(2):
                at = slice(f * 2 + z, f * 2 + z + 1)
                right_send[sweep, at] = rock[f][z][x_rows - 1 :]
                left_send[sweep, at] = coef[1][z][:1] * rock[f][z][:1]
        frac_send[sweep] = frac.astype(BF16)
        for sends, _, copy in halo_copies(sweep):
            start_when(sends, copy)

    rock = [[rock_ref[f, z] for z in range(2)] for f in range(2)]

    def to_blocks(ref):
        return jnp.concatenate(
            [ref[f : f + 1, b * LANES : (b + 1) * LANES] for f in range(2) for b in range(blocks)],
            axis=0,
        )

    frac = to_blocks(frac_ref)
    send_halos(0, rock, frac)
    loaded(9, 12, 11)

    slot_lane = lax.broadcasted_iota(jnp.int32, (1, LANES), 1)
    table_rows = 2 * x_rows * parts_y
    hot_row = lax.broadcasted_iota(jnp.int32, (LANES, LANES), 0)
    mask_row = lax.broadcasted_iota(jnp.int32, (table_rows, LANES), 0)
    block_row = lax.broadcasted_iota(jnp.int32, (blocks, LANES), 0)
    y_shift = width.bit_length() - 1
    for s in range(n):
        at = slice(s * LANES, (s + 1) * LANES)
        cell = cell_ref[0, s : s + 1, :]
        hot = jnp.where(hot_row == (cell & (LANES - 1)), 1.0, 0.0).astype(BF16)
        cell_hot[:LANES, at] = hot
        cell_hot[LANES:, at] = hot
        y_part = (cell & (width - 1)) >> 7
        table_row = y_part * (2 * x_rows) + (cell >> y_shift)
        cell_mask[:, at] = jnp.where(mask_row == table_row, 1.0, 0.0)
        weights[s : s + 1, :] = jnp.where(
            slot_lane < count_ref[0, s], weight_ref[0, s : s + 1, :], 0.0
        )

    def pick_rock(sweep, rock):
        table = jnp.concatenate(
            [
                rock[f][z][:, p * LANES : (p + 1) * LANES]
                for f in range(2) for p in range(parts_y) for z in range(2)
            ],
            axis=0,
        )
        left = jnp.concatenate(split(table), axis=1)
        for c in range(n // 2):
            at = slice(c * 256, (c + 1) * 256)
            spread = jnp.dot(left, cell_hot[:, at], preferred_element_type=F32)
            mask = cell_mask[:, at]
            for f in range(2):
                picked = jnp.sum(
                    spread[f * table_rows : (f + 1) * table_rows] * mask, axis=0, keepdims=True
                )
                for h in range(2):
                    s = 2 * c + h
                    slot_send[sweep, s, f : f + 1] = (
                        picked[:, h * LANES : (h + 1) * LANES] * weights[s : s + 1]
                    )

    def pick_frac(sweep, frac):
        left = jnp.concatenate(split(frac), axis=1)
        for c in range(n // 2):
            at = slice(c * 256, (c + 1) * 256)
            spread = jnp.dot(left, seg_hot[:, at], preferred_element_type=F32)
            mask = seg_mask[:, at]
            for f in range(2):
                picked = jnp.sum(
                    spread[f * blocks : (f + 1) * blocks] * mask, axis=0, keepdims=True
                )
                for h in range(2):
                    slot_send[sweep, 2 * c + h, 2 + f : 3 + f] = picked[
                        :, h * LANES : (h + 1) * LANES
                    ]

    def send_slots(sweep):
        def body(step, carry):
            peer = lax.rem(slab + step, n)
            pltpu.make_async_remote_copy(
                slot_send.at[sweep, peer], slot_recv.at[sweep, slab],
                slot_sems.at[0, sweep], slot_sems.at[1, sweep],
                device_id={"slab": peer}, device_id_type=MESH,
            ).start()
            return carry

        lax.fori_loop(1, n, body, 0)
        slot_recv[sweep, slab] = slot_send[sweep, slab]

    def place(values, mask_ref, hot_ref, count):
        pieces = []
        for s in range(n):
            mask = mask_ref[:, s * LANES : (s + 1) * LANES]
            parts = [split(value) for value in values(s)]
            column = [
                (parts[f][h].astype(F32) * mask).astype(BF16) for h in range(2) for f in range(2)
            ]
            pieces.append(jnp.concatenate(column, axis=0))
        left = jnp.concatenate(pieces, axis=1)
        result = lax.dot_general(left, hot_ref[:LANES, :], NT, preferred_element_type=F32)
        return result[: 2 * count] + result[2 * count :]

    pick_rock(0, rock)

    loaded(8, 5, 1)
    frac_source = to_blocks(frac_source_ref)
    my_part = slab * planes + plane
    square = (6 * blocks, 6 * blocks)
    q = lax.broadcasted_iota(jnp.int32, square, 1)
    r = lax.broadcasted_iota(jnp.int32, square, 0)
    code = jnp.zeros(square, jnp.int32)
    for k in range(3):
        for b in range(blocks):
            near = near_ref[k, b]
            owner = near // blocks
            side = jnp.where(owner > my_part, 2, jnp.where(owner < my_part, 0, 1))
            for f in range(2):
                position = side * (2 * blocks) + f * blocks + near % blocks
                code = jnp.where(r == (2 * k + f) * blocks + b, position, code)
    rim = jnp.where(q == code, 1.0, 0.0).astype(BF16)
    block_of_row = lax.broadcasted_iota(jnp.int32, (2 * blocks, LANES), 0) % blocks

    for half, sem in ((seg_send, 0), (seg_recv, 1)):
        pltpu.make_async_copy(
            half.at[pl.ds(0, n - 1)], half.at[pl.ds(0, n - 1)], seg_sems.at[sem]
        ).wait()
    for s in range(n):
        at = slice(s * LANES, (s + 1) * LANES)
        segment = seg_recv[s]
        hot = jnp.where(hot_row == (segment & (LANES - 1)), 1.0, 0.0).astype(BF16)
        seg_hot[:LANES, at] = hot
        seg_hot[LANES:, at] = hot
        seg_mask[:, at] = jnp.where(block_row == (segment >> 7), 1.0, 0.0)

    def by_block(left, right):
        total = jnp.zeros((2 * blocks, LANES), F32)
        for b in range(0, blocks, 2):
            matrices = jnp.concatenate([right(b), right(b + 1)], axis=0)
            result = lax.dot_general(left, matrices, NT, preferred_element_type=F32)
            total = jnp.where(block_of_row == b, result[:, :LANES], total)
            total = jnp.where(block_of_row == b + 1, result[:, LANES:], total)
        return total

    for sweep in range(ITERS):
        if sweep:
            pick_rock(sweep, rock)
        pick_frac(sweep, frac)
        send_slots(sweep)

        near_sum = [[None, None], [None, None]]
        for f in range(2):
            for z in range(2):
                value = rock[f][z]
                product_y = coef[2][z] * value
                product_x = coef[1][z] * value
                total = source_ref[f, z]
                total += coef[2][z] * jnp.where(lane == 0, 0.0, pltpu.roll(value, 1, 1))
                total += jnp.where(lane == width - 1, 0.0, pltpu.roll(product_y, width - 1, 1))
                total += coef[1][z] * jnp.where(row == 0, 0.0, pltpu.roll(value, 1, 0))
                total += jnp.where(
                    row == x_rows - 1, 0.0, pltpu.roll(product_x, x_rows - 1, 0)
                )
                near_sum[f][z] = total
            near_sum[f][0] += coef[0][1] * rock[f][1]
            near_sum[f][1] += coef[0][1] * rock[f][0]

        if sweep == 0:
            loaded(6, 7, 3)
        copies = halo_copies(sweep)
        for _, lands, copy in copies:
            landed_when(lands, copy)
        for f in range(2):
            near_sum[f][0] += coef[0][0] * up_recv[sweep, f]
            near_sum[f][1] += down_recv[sweep, f]
            for z in range(2):
                at = slice(f * 2 + z, f * 2 + z + 1)
                near_sum[f][z] += jnp.where(
                    row == 0, coef[1][z] * right_recv[sweep, at],
                    jnp.where(row == x_rows - 1, left_recv[sweep, at], 0.0),
                )
        around = jnp.concatenate(
            [below_recv[sweep], frac.astype(BF16), above_recv[sweep]], axis=0
        )
        gathered = jnp.dot(rim, around, preferred_element_type=F32).astype(BF16)
        gathered = jnp.concatenate(
            [gathered[k * 2 * blocks : (k + 1) * 2 * blocks] for k in range(3)], axis=1
        )
        coupled = by_block(
            gathered, lambda b: jnp.concatenate([coupling_ref[b, k] for k in range(3)], axis=1)
        )

        pltpu.make_async_copy(
            slot_recv.at[sweep, pl.ds(0, n - 1)], slot_recv.at[sweep, pl.ds(0, n - 1)],
            slot_sems.at[1, sweep],
        ).wait()
        leak_frac = place(
            lambda s: [slot_recv[sweep, s, f : f + 1] for f in range(2)], seg_mask, seg_hot, blocks
        )
        frac_rhs = (frac_source + leak_frac - coupled).astype(BF16)
        frac = by_block(frac_rhs, lambda b: frac_inverse_ref[b])
        leak_rock = place(
            lambda s: [
                weights[s : s + 1] * slot_recv[sweep, s, 2 + f : 3 + f] for f in range(2)
            ],
            cell_mask, cell_hot, table_rows,
        )
        rhs = [[None, None], [None, None]]
        for f in range(2):
            for z in range(2):
                first = [f * table_rows + (p * 2 + z) * x_rows for p in range(parts_y)]
                rhs[f][z] = near_sum[f][z] + jnp.concatenate(
                    [leak_rock[i : i + x_rows] for i in first], axis=1
                )
        rock = [
            [
                inverse_ref[2 * g, z].astype(F32) * rhs[0][z]
                + inverse_ref[2 * g + 1, z].astype(F32) * rhs[1][z]
                for z in range(2)
            ]
            for g in range(2)
        ]
        if sweep < ITERS - 1:
            send_halos(sweep + 1, rock, frac)

    for f in range(2):
        for z in range(2):
            rock_out[f, z] = rock[f][z]
        for b in range(blocks):
            frac_out[f : f + 1, b * LANES : (b + 1) * LANES] = frac[
                f * blocks + b : f * blocks + b + 1
            ]
    for sweep in range(ITERS):
        for sends, _, copy in halo_copies(sweep):
            sent_when(sends, copy)
        pltpu.make_async_copy(
            slot_send.at[sweep, pl.ds(0, n - 1)], slot_send.at[sweep, pl.ds(0, n - 1)],
            slot_sems.at[0, sweep],
        ).wait()


def shards(n, planes, *operands):
    operands = operands[:8] + (operands[8].T,) + operands[9:]
    rock_state = operands[0]
    blocks = operands[6].shape[0]
    _, layers, x_rows, width = rock_state.shape
    table_rows = layers * x_rows * width // LANES
    vmem = pl.BlockSpec(memory_space=pltpu.VMEM)
    hbm = pl.BlockSpec(memory_space=pltpu.HBM)
    scalars = (8, 12)
    slots = n * LANES
    return pl.pallas_call(
        functools.partial(kernel, n, planes),
        out_shape=(
            jax.ShapeDtypeStruct(rock_state.shape, F32),
            jax.ShapeDtypeStruct(operands[4].shape, F32),
        ),
        in_specs=[hbm] * len(operands),
        out_specs=(vmem, vmem),
        scratch_shapes=[
            (pltpu.SMEM if i in scalars else pltpu.VMEM)(array.shape, array.dtype)
            for i, array in enumerate(operands)
        ]
        + [
            pltpu.VMEM((2 * LANES, slots), BF16),
            pltpu.VMEM((table_rows, slots), F32),
            pltpu.VMEM((2 * LANES, slots), BF16),
            pltpu.VMEM((blocks, slots), F32),
            pltpu.VMEM((n, LANES), F32),
            pltpu.VMEM((n, 1, LANES), jnp.int32),
            pltpu.VMEM((n, 1, LANES), jnp.int32),
            pltpu.VMEM((ITERS, n, 4, LANES), F32),
            pltpu.VMEM((ITERS, n, 4, LANES), F32),
            pltpu.VMEM((ITERS, 2, x_rows, width), F32),
            pltpu.VMEM((ITERS, 2, x_rows, width), F32),
            pltpu.VMEM((ITERS, 2, x_rows, width), F32),
            pltpu.VMEM((ITERS, 2, x_rows, width), F32),
            pltpu.VMEM((ITERS, 2 * layers, width), F32),
            pltpu.VMEM((ITERS, 2 * layers, width), F32),
            pltpu.VMEM((ITERS, 2 * layers, width), F32),
            pltpu.VMEM((ITERS, 2 * layers, width), F32),
            pltpu.VMEM((ITERS, 2 * blocks, LANES), BF16),
            pltpu.VMEM((ITERS, 2 * blocks, LANES), BF16),
            pltpu.VMEM((ITERS, 2 * blocks, LANES), BF16),
            pltpu.SemaphoreType.DMA((2,)),
            pltpu.SemaphoreType.DMA((2, ITERS)),
            pltpu.SemaphoreType.DMA((6, ITERS)),
            pltpu.SemaphoreType.DMA((6, ITERS)),
            pltpu.SemaphoreType.DMA((len(operands),)),
        ],
        compiler_params=pltpu.CompilerParams(
            collective_id=0, has_side_effects=True, vmem_limit_bytes=127 * 512 * 1024
        ),
    )(*operands)


def solution(mesh):
    return jax.shard_map(
        functools.partial(shards, mesh.shape["slab"], mesh.shape["plane"]),
        mesh=mesh,
        in_specs=(
            P(None, "slab", "plane", None),
            P(None, "slab", "plane", None),
            P(None, "slab", "plane", None),
            P(None, "slab", "plane", None),
            P(None, ("slab", "plane")),
            P(None, ("slab", "plane")),
            P(("slab", "plane"), None, None, None),
            P(("slab", "plane"), None, None),
            P(("slab", "plane"), None),
            P("slab", "plane", None),
            P("slab", "plane", None),
            P("slab", "plane", None),
            P("slab", "plane"),
        ),
        out_specs=(P(None, "slab", "plane", None), P(None, ("slab", "plane"))),
        check_vma=False,
    )
```
